256 devices in a mesh: req: 32 (over y, z), head: 8 (over x, core).
Axes of the slice: x: 4, y: 4, z: 8, core: 2. Of those that a mesh axis runs over, the one named last changes fastest.
Arguments:
- kv_pool: bfloat16 [5120, 8, 128, 256], P('req', 'head'), may hold values from -6 to 6
- block_table: int32 [1024, 5], P('req'), may hold values from 0 to 159, as said below
- lengths: int32 [1024], replicated, may hold values from 1 to 640, as said below
- new_slot: int32 [1024], replicated, may hold values from 0 to 1023, as said below
- queries: bfloat16 [1024, 2, 8192], P('req', None, 'head'), may hold values from -200 to 200
- new_kv: bfloat16 [1024, 2, 8, 256], P('req', None, 'head'), may hold values from -8 to 8
- output_weight: bfloat16 [8192, 8192], P('head', 'req'), may hold values from -0.0625 to 0.0625
- residual: bfloat16 [1024, 2, 8192], P('head', None, 'req'), may hold values from -6 to 6
Outputs:
- hidden_out: bfloat16 [1024, 2, 8192], P('head', None, 'req')
The draws below stay inside these ranges and needn't reach their ends.
Inputs may be any that keep to these rules, and one draw needn't show every extreme that they name: `lengths`: on each of a quarter of the devices some request holds exactly 640 tokens. `new_slot`: A permutation made of swaps: device d trades exactly 2 requests with device (d + 32 / 2) mod 32, or none, half of the devices trading; a request that changes device holds at most 4 pages, and on some devices each of the 2 traded requests holds exactly 4 pages. `block_table`: pages of one device's requests are distinct pages of that device's 160; entries past a request's last page are 0 and unused.
All inputs are finite; a program needn't handle non-finite values.
Results may differ from the reference program's by a relative error of at most 0.0075.
Values may be sent and summed in bfloat16 or wider, within the bound.
A program may use at most 128 MiB of HBM per device.

```python
import math
import jax
import jax.numpy as jnp
from jax import lax

D = 8192
QH = 64
KVH = 8
HD = 128
PAGE = 128
MAXP = 5
MOVE_PAGES = 4
SWAP = 2
STEPS = 2
R_DEV = 32
QD = 8192
REQS = 1024
P_DEV = 160
POOL = 5120
N_REQ = 32


def plan(key):
    devices_all = REQS // R_DEV
    half_count = devices_all // 2
    key_perm, key_slots, key_pages, key_tail, key_pool = jax.random.split(key, 5)
    own_dev = jnp.arange(devices_all, dtype=jnp.int32)
    partner = (own_dev + half_count) % devices_all
    pair_id = own_dev % half_count
    pair_perm = jax.random.permutation(key_perm, half_count).astype(jnp.int32)
    trading = (pair_perm[pair_id] - pair_perm[half_count - 1]) % half_count < half_count // 2
    flips = jax.random.randint(jax.random.fold_in(key_perm, 1), (half_count,), 0, 2).astype(jnp.int32)
    upper = (own_dev >= half_count).astype(jnp.int32)
    heavy_dev = trading & (upper == flips[pair_id])
    slot_permutation = jax.vmap(lambda sub: jax.random.permutation(sub, R_DEV))(jax.random.split(key_slots, devices_all)).astype(jnp.int32)
    rank = jnp.argsort(slot_permutation, axis=1).astype(jnp.int32)
    moved = trading[:, None] & (rank < SWAP)
    heavy = jnp.broadcast_to(heavy_dev[:, None], (devices_all, R_DEV))
    page_count = jax.random.randint(key_pages, (devices_all, R_DEV), MAXP - 1, MAXP + 1).astype(jnp.int32)
    page_count = jnp.where(heavy, page_count, 1)
    longest = heavy & (rank == SWAP)
    page_count = jnp.where(longest, MAXP, page_count)
    page_count = jnp.where(moved & heavy, MOVE_PAGES, page_count)
    tail = jax.random.randint(key_tail, (devices_all, R_DEV), 1, PAGE + 1).astype(jnp.int32)
    tail = jnp.where(longest, PAGE, tail)
    lengths = (page_count - 1) * PAGE + tail
    own_slot = own_dev[:, None] * R_DEV + jnp.arange(R_DEV, dtype=jnp.int32)[None, :]
    other_slot = partner[:, None] * R_DEV + jnp.take_along_axis(slot_permutation[partner], rank, axis=1)
    new_slot = jnp.where(moved, other_slot, own_slot).astype(jnp.int32)
    pool_perm = jax.vmap(lambda sub: jax.random.permutation(sub, P_DEV))(jax.random.split(key_pool, devices_all)).astype(jnp.int32)
    offsets = jnp.cumsum(page_count, axis=1) - page_count
    page_index = offsets[:, :, None] + jnp.arange(MAXP, dtype=jnp.int32)[None, None, :]
    valid = jnp.arange(MAXP, dtype=jnp.int32)[None, None, :] < page_count[:, :, None]
    looked = jax.vmap(lambda perm_row, idx_rows: perm_row[idx_rows])(pool_perm, jnp.minimum(page_index, P_DEV - 1))
    table = jnp.where(valid, looked, 0).astype(jnp.int32)
    return (lengths.reshape(REQS), table.reshape(REQS, MAXP), new_slot.reshape(REQS))


def draw_lengths(key, part):
    drawn = plan(key)
    return drawn[0]


def draw_block_table(key, part):
    drawn = plan(key)
    return drawn[1]


def draw_new_slot(key, part):
    drawn = plan(key)
    return drawn[2]


def draw_queries(key, part):
    key = jax.random.fold_in(key, 3)
    base = jnp.clip(jax.random.normal(key, (REQS, STEPS, QH * HD), jnp.float32), -6.0, 6.0)
    return base.astype(jnp.bfloat16)


def draw_new_kv(key, part):
    key = jax.random.fold_in(key, 5)
    base = jnp.clip(jax.random.normal(key, (REQS, STEPS, KVH, 2 * HD), jnp.float32), -6.0, 6.0)
    return base.astype(jnp.bfloat16)


def shard_levels(rng, extent, cuts, least, largest):
    level, own = 1.0, jax.random.fold_in(rng, 6)
    for axis_at, blocks in cuts:
        steps = jnp.exp(jax.random.uniform(jax.random.fold_in(own, axis_at), (blocks,), jnp.float32, least / len(cuts), largest / len(cuts)))
        level = level * jnp.repeat(steps, extent[axis_at] // blocks).reshape([-1 if axis == axis_at else 1 for axis in range(len(extent))])
    return level


def normal_values(key, shape, spread, reach, cuts=(), held_as=jnp.bfloat16):
    factor_of = shard_levels(key, shape, cuts, -0.22, 0.18) if cuts else 1.0
    values = jax.random.normal(key, shape, jnp.float32) * spread * factor_of
    return jnp.minimum(jnp.maximum(values, -reach), reach).astype(held_as)


def setup_inputs(seed: int = 0) -> dict:
    seeds = jax.random.split(jax.random.key(seed), 9)
    kv_pool = normal_values(seeds[0], (POOL, KVH, PAGE, 2 * HD), 1.0, 6.0, ((0, 32), (1, 8)))
    block_table = draw_block_table(jax.random.fold_in(seeds[8], 71), 0)
    lengths = draw_lengths(jax.random.fold_in(seeds[8], 71), 0)
    new_slot = draw_new_slot(jax.random.fold_in(seeds[8], 71), 0)
    queries = draw_queries(jax.random.fold_in(seeds[8], 71), 0)
    new_kv = draw_new_kv(jax.random.fold_in(seeds[8], 71), 0)
    output_weight = normal_values(seeds[6], (QD, D), QD ** -0.5, 0.0625, ((0, 8), (1, 32)))
    residual = normal_values(seeds[7], (REQS, STEPS, D), 1.0, 6.0, ((0, 8), (2, 32)))
    return {"kv_pool": kv_pool, "block_table": block_table, "lengths": lengths, "new_slot": new_slot, "queries": queries, "new_kv": new_kv, "output_weight": output_weight, "residual": residual}


NEG_FILL = -1e+30

def device_block(device, kv_pool, block_table, lengths, new_slot, queries, new_kv):
    first_slot = device * R_DEV
    pool_part = lax.dynamic_slice_in_dim(kv_pool, device * P_DEV, P_DEV, 0)
    table_share = lax.dynamic_slice_in_dim(block_table, first_slot, R_DEV, 0)
    length_share = lax.dynamic_slice_in_dim(lengths, first_slot, R_DEV, 0)
    target = lax.dynamic_slice_in_dim(new_slot, first_slot, R_DEV, 0)
    paged = pool_part[table_share]
    cached = jnp.transpose(paged, (0, 2, 1, 3, 4)).reshape(R_DEV, KVH, MAXP * PAGE, 2 * HD).astype(jnp.float32)
    query_rows = queries[target].astype(jnp.float32).reshape(R_DEV, STEPS, KVH, QH // KVH, HD)
    fresh = new_kv[target].astype(jnp.float32)
    scaling = 1.0 / math.sqrt(HD)
    cache_scores = jnp.einsum('rskgd,rktd->rskgt', query_rows, cached[..., :HD]) * scaling
    positions = jnp.arange(MAXP * PAGE)
    valid = positions[None, :] < length_share[:, None]
    cache_scores = jnp.where(valid[:, None, None, None, :], cache_scores, NEG_FILL)
    fresh_scores = jnp.einsum('rskgd,rukd->rskgu', query_rows, fresh[..., :HD]) * scaling
    causal = jnp.arange(STEPS)[None, :] <= jnp.arange(STEPS)[:, None]
    fresh_scores = jnp.where(causal[None, :, None, None, :], fresh_scores, NEG_FILL)
    top = jnp.maximum(lax.optimization_barrier(jnp.max(cache_scores, -1)), lax.optimization_barrier(jnp.max(fresh_scores, -1)))
    cache_weights = jnp.exp(cache_scores - top[..., None])
    fresh_weights = jnp.exp(fresh_scores - top[..., None])
    total = lax.optimization_barrier(jnp.sum(cache_weights, -1)) + lax.optimization_barrier(jnp.sum(fresh_weights, -1))
    cache_low = lax.optimization_barrier(cache_weights.astype(jnp.bfloat16))
    fresh_low = lax.optimization_barrier(fresh_weights.astype(jnp.bfloat16))
    mixed = jnp.einsum('rskgt,rktd->rskgd', cache_low.astype(jnp.float32), cached[..., HD:])
    mixed = mixed + jnp.einsum('rskgu,rukd->rskgd', fresh_low.astype(jnp.float32), fresh[..., HD:])
    return (mixed / total[..., None]).reshape(R_DEV, STEPS, QH * HD).astype(jnp.bfloat16)

def reference(kv_pool, block_table, lengths, new_slot, queries, new_kv, output_weight, residual):
    blocks = lax.map(lambda device: device_block(device, kv_pool, block_table, lengths, new_slot, queries, new_kv), jnp.arange(N_REQ, dtype=jnp.int32))
    attended_old = blocks.reshape(REQS, STEPS, QH * HD)
    attended = jnp.zeros_like(attended_old).at[new_slot].set(attended_old)
    flat = attended.reshape(REQS * STEPS, QH * HD)
    projected = jnp.dot(flat, output_weight, preferred_element_type=jnp.float32).reshape(REQS, STEPS, D)
    return (residual.astype(jnp.float32) + projected).astype(jnp.bfloat16)
```

```python
import functools
import math

import jax
import jax.numpy as jnp
from jax import lax
from jax.experimental import pallas as pl
from jax.experimental.pallas import tpu as pltpu
from jax.sharding import PartitionSpec as P

MESH = pl.DeviceIdType.MESH
NEG_FILL = -1e30
NT = (((1,), (1,)), ((), ()))
NN = (((1,), (0,)), ((), ()))


def dot(a, b, dims=NN):
    return lax.dot_general(a, b, dims, preferred_element_type=jnp.float32)


def scan_leaving(new_slot, device):
    def body(e, carry):
        count, i0, i1, t0, t1 = carry
        v = new_slot[device * 32 + e]
        leaves = jnp.where((v >> 5) != device, 1, 0)
        first = (leaves == 1) & (count == 0)
        second = (leaves == 1) & (count == 1)
        return (
            count + leaves,
            jnp.where(first, e, i0),
            jnp.where(second, e, i1),
            jnp.where(first, v & 31, t0),
            jnp.where(second, v & 31, t1),
        )

    zero = jnp.int32(0)
    return lax.fori_loop(
        0, 32, body, (zero, zero, zero, jnp.int32(30), jnp.int32(31)), unroll=4
    )


def kernel(
    pool, weight, queries, fresh2, fresh3, residual, table, lengths, new_slot, out,
    pool_v, w_v, q_v, f2_v, f3_v, res_v, fv_v, att_v, attended, qx_s, qx_r, ret_s, ret_r,
    c_s, c_r, own_v, y_s, y_r, x_r, perm_v,
    l_sem, qx_sem, ret_sem, w_ss, w_rs, z_ss, z_rs, c_ss, c_rs, y_ss, y_rs, x_ss, x_rs,
):
    req, head = lax.axis_index("req"), lax.axis_index("head")
    x, core = head // 2, head % 2
    y, z = req // 8, req % 8
    partner = (req + 16) % 32

    def at(dx=0, dy=0, dz=0, flip=0):
        return (
            ((y + dy) % 4) * 8 + (z + dz) % 8,
            ((x + dx) % 4) * 2 + (core + flip) % 2,
        )

    def remote(src, dst, ss, rs, device):
        return pltpu.make_async_remote_copy(
            src_ref=src, dst_ref=dst, send_sem=ss, recv_sem=rs,
            device_id=device, device_id_type=MESH,
        )

    barrier = pltpu.get_barrier_semaphore()
    peers = [at(dz=d) for d in (1, 7, 2, 6)]
    peers += [at(dy=d) for d in (1, 3, 2)]
    peers += [at(dx=d) for d in (1, 3, 2)]
    peers += [at(flip=1)]
    for peer in peers:
        pl.semaphore_signal(barrier, inc=1, device_id=peer, device_id_type=MESH)

    load_q = pltpu.make_async_copy(queries, q_v, l_sem.at[0])
    load_f2 = pltpu.make_async_copy(fresh2, f2_v, l_sem.at[1])
    load_f3 = pltpu.make_async_copy(fresh3, f3_v, l_sem.at[2])
    load_w = pltpu.make_async_copy(weight, w_v.at[0], l_sem.at[3])
    load_pool = pltpu.make_async_copy(pool, pool_v, l_sem.at[4])
    load_res = pltpu.make_async_copy(residual, res_v, l_sem.at[5])
    for load in (load_q, load_f2, load_f3, load_w, load_pool, load_res):
        load.start()

    _, i0, i1, _, _ = scan_leaving(new_slot, req)
    trades, _, _, t0, t1 = scan_leaving(new_slot, partner)
    low, high = jnp.minimum(t0, t1), jnp.maximum(t0, t1)

    load_q.wait()
    load_f2.wait()
    load_f3.wait()
    for k, t in enumerate((t0, t1)):
        new_rows = f3_v[t].astype(jnp.float32)
        qx_s[k, 0:16] = q_v[t]
        qx_s[k, 16:32] = jnp.concatenate(
            [new_rows, jnp.zeros((12, 128), jnp.float32)], 0
        ).astype(jnp.bfloat16)
        qx_s[k, 32:48] = jnp.concatenate(
            [new_rows[2:4], jnp.zeros((14, 128), jnp.float32)], 0
        ).astype(jnp.bfloat16)
    fv_v[...] = pltpu.roll(f2_v[...].astype(jnp.float32), 126, 0).astype(jnp.bfloat16)

    pl.semaphore_wait(barrier, len(peers))

    send_q = remote(qx_s, qx_r, qx_sem.at[0], qx_sem.at[1], at(dy=2))
    send_q.start()
    load_w.wait()

    def w_half(d, half):
        return w_v.at[d, pl.ds(half * 512, 512)]

    w_plan = [(0, 3, 1, 0), (1, 1, 3, 1), (1, 3, 1, 2), (0, 1, 3, 3)]
    w_own = [
        remote(w_half(0, half), w_half(d, half), w_ss.at[k], w_rs.at[k], at(dy=dy))
        for half, d, dy, k in w_plan
    ]
    w_own[0].start()
    w_own[1].start()

    t_row = lax.broadcasted_iota(jnp.int32, (128, 256), 0)
    u_col = lax.broadcasted_iota(jnp.int32, (128, 256), 1) & 63
    slot_t = t_row >> 2
    for q in range(4):
        source = x * 8 + core * 4 + q
        _, _, _, a, b = scan_leaving(new_slot, (source + 16) % 32)
        lo, hi = jnp.minimum(a, b), jnp.maximum(a, b)
        last = jnp.where(hi == 30, lo, hi)
        pos = jnp.where(slot_t == 30, lo, slot_t)
        pos = jnp.where(slot_t == 31, last, pos)
        pos = jnp.where(slot_t == lo, 30, pos)
        pos = jnp.where(slot_t == hi, 31, pos)
        row = ((pos >> 3) << 4) + ((t_row & 1) << 3) + (pos & 7)
        for ct in range(2):
            hit = (row == u_col) & (((t_row >> 1) & 1) == ct)
            perm_v[q, ct] = jnp.where(hit, 1.0, 0.0).astype(jnp.bfloat16)

    load_pool.wait()

    scaling = 1.0 / math.sqrt(128)
    lane = lax.broadcasted_iota(jnp.int32, (16, 128), 1)
    odd = (lax.broadcasted_iota(jnp.int32, (16, 128), 0) & 1) == 1

    def attend(query, old, keys_new, values_new, place):
        span = lengths[req * 32 + old]
        pages = [table[p, old] for p in range(5)]
        scores = []
        for p in range(5):
            s = dot(query, pool_v[pages[p], :, 0:128], NT) * scaling
            scores.append(jnp.where(lane < span - 128 * p, s, NEG_FILL))
        s = dot(query, keys_new, NT) * scaling
        seen = (lane == place) | ((lane == place + 1) & odd)
        scores.append(jnp.where(seen, s, NEG_FILL))
        top = functools.reduce(jnp.maximum, scores)
        top = jnp.max(top, axis=1, keepdims=True)
        weights = [jnp.exp(s - top) for s in scores]
        total = jnp.sum(functools.reduce(jnp.add, weights), axis=1, keepdims=True)
        mixed = dot(weights[5].astype(jnp.bfloat16), values_new)
        for p in range(5):
            mixed += dot(weights[p].astype(jnp.bfloat16), pool_v[pages[p], :, 128:256])
        return mixed / total

    def slot_at(p):
        slot = jnp.where(p == low, jnp.where(high == 30, 31, 30), p)
        slot = jnp.where(p == high, 31, slot)
        slot = jnp.where(p == 30, low, slot)
        return jnp.where(p == 31, high, slot)

    def group(c):
        for k in range(8):
            slot = slot_at(jnp.int32(c * 8 + k))
            v = new_slot[req * 32 + slot]
            old = jnp.where((v >> 5) == req, v & 31, slot)
            att_v[k * 16 : k * 16 + 16] = attend(
                q_v[slot], old, f2_v[...], fv_v[...], slot * 4
            )

    def chunk(c):
        return attended.at[z, pl.ds(c * 16, 16)]

    def block(dz, c):
        return attended.at[(z + dz) % 8, pl.ds(c * 16, 16)]

    def publish(c):
        for g in range(8):
            rows = [att_v[pl.ds(2 * g + s, 8, stride=16)] for s in range(2)]
            attended[z, c * 16 : c * 16 + 16, g * 128 : g * 128 + 128] = (
                jnp.concatenate(rows, 0).astype(jnp.bfloat16)
            )
        sends = [
            remote(chunk(c), chunk(c), z_ss.at[c, k], z_rs.at[c, k], at(dz=dz))
            for k, dz in enumerate((1, 7, 2, 6))
        ]
        for k in (2, 3, 0, 1):
            sends[k].start()
        return sends

    def arrive(dz, c, k):
        remote(block(dz, c), block(dz, c), z_ss.at[c, k], z_rs.at[c, k], at(dz=1)).wait_recv()

    def forward(c):
        sends = []
        arrive(6, c, 2)
        sends.append(remote(block(6, c), block(6, c), z_ss.at[c, 4], z_rs.at[c, 4], at(dz=1)))
        if c % 2 == 0:
            sends.append(
                remote(block(6, c), block(6, c), z_ss.at[c, 6], z_rs.at[c, 6], at(dz=2))
            )
        for send in sends:
            send.start()
        arrive(2, c, 3)
        more = [remote(block(2, c), block(2, c), z_ss.at[c, 5], z_rs.at[c, 5], at(dz=7))]
        if c % 2 == 1:
            more.append(
                remote(block(2, c), block(2, c), z_ss.at[c, 6], z_rs.at[c, 6], at(dz=6))
            )
        for send in more:
            send.start()
        return sends + more

    z_sends = []
    group(0)
    z_sends += publish(0)

    send_q.wait_recv()
    pad = jnp.zeros((112, 128), jnp.bfloat16)
    for k, old in enumerate((i0, i1)):
        result = attend(
            qx_r[k, 0:16], old,
            jnp.concatenate([qx_r[k, 16:32], pad], 0),
            jnp.concatenate([qx_r[k, 32:48], pad], 0),
            0,
        )
        ret_s[k] = result.astype(jnp.bfloat16)
    send_ret = remote(ret_s, ret_r, ret_sem.at[0], ret_sem.at[1], at(dy=2))
    send_ret.start()
    w_own[2].start()
    w_own[3].start()

    group(1)
    z_sends += publish(1)
    group(2)
    z_sends += publish(2)
    group(3)
    z_sends += forward(0)
    send_ret.wait_recv()
    for p, t in ((6, low), (7, high)):
        came = ret_r[jnp.where(t == t0, 0, 1)].astype(jnp.float32)
        att_v[p * 16 : p * 16 + 16] = jnp.where(
            trades > 0, came, att_v[p * 16 : p * 16 + 16]
        )
    z_sends += publish(3)

    w_fwd = []
    for half, d, dy, k, came in ((0, 3, 1, 4, 0), (1, 1, 3, 5, 1)):
        w_own[came].wait_recv()
        w_fwd.append(
            remote(w_half(d, half), w_half(2, half), w_ss.at[k], w_rs.at[k], at(dy=dy))
        )
        w_fwd[-1].start()
    for c in (1, 2, 3):
        z_sends += forward(c)
    for c in range(4):
        arrive(7, c, 0)
        arrive(1, c, 1)
        arrive(5, c, 4)
        arrive(3, c, 5)
        arrive(4, c, 6)

    def rows_of(which):
        return attended[pl.ds(which * 4, 4)].reshape(256, 1024)

    def core_copy(d):
        return remote(c_s.at[d], c_r.at[d], c_ss.at[d], c_rs.at[d], at(flip=1))

    def y_copy(d):
        return remote(y_s.at[d], y_r.at[d], y_ss.at[d], y_rs.at[d], at(dy=d))

    def product(which, d):
        return dot(rows_of(which), w_v[d])

    def away(d):
        c_s[d] = product(1 - core, d).astype(jnp.bfloat16)
        core_copy(d).start()

    def near(d):
        own_v[d] = product(core, d)

    def join(d):
        core_copy(d).wait_recv()
        both = own_v[d] + c_r[d].astype(jnp.float32)
        both = both.astype(jnp.bfloat16).reshape(4, 64, 256)
        if d == 0:
            y_r[0] = both
        else:
            y_s[d] = both
            y_copy(d).start()

    def x_move(d):
        i = (y + 4 - d) % 4
        far = remote(y_r.at[d], x_r.at[:, x], x_ss.at[d], x_rs.at[x], (req, i * 2 + core))
        here = pltpu.make_async_copy(y_r.at[d], x_r.at[:, x], x_ss.at[d])
        return i != x, far, here

    def x_start(d):
        other, far, here = x_move(d)

        @pl.when(other)
        def _():
            far.start()

        @pl.when(jnp.logical_not(other))
        def _():
            here.start()

    w_own[2].wait_recv()
    w_own[3].wait_recv()
    for d in (1, 3, 0):
        away(d)
    for d in (1, 3, 0):
        near(d)
    for d in (1, 3):
        join(d)
    for k in (4, 5):
        w_fwd[k - 4].wait_recv()
    away(2)
    near(2)
    join(0)
    x_start(0)
    join(2)
    for d in (1, 3, 2):
        y_copy(d).wait_recv()
        x_start(d)

    for d in range(4):
        other, far, here = x_move(d)

        @pl.when(other)
        def _():
            far.wait_send()

        @pl.when(jnp.logical_not(other))
        def _():
            here.wait()

    for k in range(4):

        @pl.when(k != x)
        def _():
            remote(
                y_r.at[0], x_r.at[:, k], x_ss.at[0], x_rs.at[k], at(dx=1)
            ).wait_recv()

    load_res.wait()
    for q in range(4):
        parts = x_r[q].reshape(256, 256)
        total = dot(perm_v[q, 0], parts[:, 0:128]) + dot(perm_v[q, 1], parts[:, 128:256])
        total += res_v[q * 128 : q * 128 + 128].astype(jnp.float32)
        out[q * 128 : q * 128 + 128] = total.astype(jnp.bfloat16)

    send_q.wait_send()
    send_ret.wait_send()
    for send in w_own + w_fwd + z_sends:
        send.wait_send()
    for d in range(4):
        core_copy(d).wait_send()
    for d in (1, 2, 3):
        y_copy(d).wait_send()


def per_device(kv_pool, block_table, lengths, new_slot, queries, new_kv, output_weight, residual):
    q = queries.reshape(32, 2, 8, 128).transpose(0, 2, 1, 3).reshape(32, 16, 128)
    fresh = new_kv.reshape(32, 2, 2, 128).transpose(0, 2, 1, 3)
    res = residual.reshape(128, 2, 2, 128).transpose(0, 2, 1, 3).reshape(512, 128)
    hbm = pl.BlockSpec(memory_space=pl.ANY)
    smem = pl.BlockSpec(memory_space=pltpu.SMEM)
    vmem = pl.BlockSpec(memory_space=pltpu.VMEM)
    bf16, f32 = jnp.bfloat16, jnp.float32
    sem = pltpu.SemaphoreType.DMA
    out = pl.pallas_call(
        kernel,
        name="decode",
        out_shape=jax.ShapeDtypeStruct((512, 128), bf16),
        in_specs=[hbm] * 6 + [smem] * 3,
        out_specs=vmem,
        scratch_shapes=[
            pltpu.VMEM((160, 128, 256), bf16),
            pltpu.VMEM((4, 1024, 256), bf16),
            pltpu.VMEM((32, 16, 128), bf16),
            pltpu.VMEM((128, 128), bf16),
            pltpu.VMEM((32, 4, 128), bf16),
            pltpu.VMEM((512, 128), bf16),
            pltpu.VMEM((128, 128), bf16),
            pltpu.VMEM((128, 128), f32),
            pltpu.VMEM((8, 64, 1024), bf16),
            pltpu.VMEM((2, 48, 128), bf16),
            pltpu.VMEM((2, 48, 128), bf16),
            pltpu.VMEM((2, 16, 128), bf16),
            pltpu.VMEM((2, 16, 128), bf16),
            pltpu.VMEM((4, 256, 256), bf16),
            pltpu.VMEM((4, 256, 256), bf16),
            pltpu.VMEM((4, 256, 256), f32),
            pltpu.VMEM((4, 4, 64, 256), bf16),
            pltpu.VMEM((4, 4, 64, 256), bf16),
            pltpu.VMEM((4, 4, 64, 256), bf16),
            pltpu.VMEM((4, 2, 128, 256), bf16),
            sem((6,)),
            sem((2,)),
            sem((2,)),
            sem((6,)),
            sem((6,)),
            sem((4, 7)),
            sem((4, 7)),
            sem((4,)),
            sem((4,)),
            sem((4,)),
            sem((4,)),
            sem((4,)),
            sem((4,)),
        ],
        compiler_params=pltpu.CompilerParams(
            collective_id=0, has_side_effects=True, vmem_limit_bytes=48 << 20
        ),
    )(
        kv_pool.reshape(160, 128, 256), output_weight, q, fresh.reshape(128, 128),
        fresh.reshape(32, 4, 128), res, block_table.T, lengths, new_slot,
    )
    return out.reshape(128, 2, 2, 128).transpose(0, 2, 1, 3).reshape(128, 2, 256)


def solution(mesh):
    in_specs = (
        P("req", "head", None, None),
        P("req", None),
        P(),
        P(),
        P("req", None, "head"),
        P("req", None, "head", None),
        P("head", "req"),
        P("head", None, "req"),
    )
    return jax.shard_map(
        per_device, mesh=mesh, in_specs=in_specs,
        out_specs=P("head", None, "req"), check_vma=False,
    )
```

```python
import functools
import math

import jax
import jax.numpy as jnp
from jax import lax
from jax.experimental import pallas as pl
from jax.experimental.pallas import tpu as pltpu
from jax.sharding import PartitionSpec as P

MESH = pl.DeviceIdType.MESH
NEG_FILL = -1e30
NT = (((1,), (1,)), ((), ()))
NN = (((1,), (0,)), ((), ()))


def dot(a, b, dims=NN):
    return lax.dot_general(a, b, dims, preferred_element_type=jnp.float32)


def scan_leaving(new_slot, device):
    def body(e, carry):
        count, i0, i1, t0, t1 = carry
        v = new_slot[device * 32 + e]
        leaves = jnp.where((v >> 5) != device, 1, 0)
        first = (leaves == 1) & (count == 0)
        second = (leaves == 1) & (count == 1)
        return (
            count + leaves,
            jnp.where(first, e, i0),
            jnp.where(second, e, i1),
            jnp.where(first, v & 31, t0),
            jnp.where(second, v & 31, t1),
        )

    zero = jnp.int32(0)
    return lax.fori_loop(
        0, 32, body, (zero, zero, zero, jnp.int32(30), jnp.int32(31)), unroll=4
    )


def kernel(
    pool, weight, queries, fresh2, fresh3, residual, table, lengths, new_slot, out,
    pool_v, w_v, q_v, f2_v, f3_v, res_v, fv_v, att_v, attended, qx_s, qx_r, ret_s, ret_r,
    c_s, c_r, own_v, y_s, y_r, x_r, perm_v,
    l_sem, qx_sem, ret_sem, w_ss, w_rs, z_ss, z_rs, c_ss, c_rs, y_ss, y_rs, x_ss, x_rs, ready,
):
    req, head = lax.axis_index("req"), lax.axis_index("head")
    x, core = head // 2, head % 2
    y, z = req // 8, req % 8
    partner = (req + 16) % 32

    def at(dx=0, dy=0, dz=0, flip=0):
        return (
            ((y + dy) % 4) * 8 + (z + dz) % 8,
            ((x + dx) % 4) * 2 + (core + flip) % 2,
        )

    def remote(src, dst, ss, rs, device):
        return pltpu.make_async_remote_copy(
            src_ref=src, dst_ref=dst, send_sem=ss, recv_sem=rs,
            device_id=device, device_id_type=MESH,
        )

    barrier = pltpu.get_barrier_semaphore()
    for peer in [at(dy=d) for d in (1, 3, 2)] + [at(dx=d) for d in (1, 3, 2)] + [at(flip=1)]:
        pl.semaphore_signal(barrier, inc=1, device_id=peer, device_id_type=MESH)

    def rank_of(place):
        return place - (place // 4) * (place - 4)

    rank = rank_of(z)
    ahead = [rank - rank_of((z + d) % 8) for d in (1, 7, 2, 6)]
    before = sum((a + 8) // 8 for a in ahead)
    behind = 4 - before
    for d, a in zip((1, 7, 2, 6), ahead):

        @pl.when(a <= 0)
        def _():
            pl.semaphore_signal(barrier, inc=1, device_id=at(dz=d), device_id_type=MESH)

    load_q = pltpu.make_async_copy(queries, q_v, l_sem.at[0])
    load_f2 = pltpu.make_async_copy(fresh2, f2_v, l_sem.at[1])
    load_f3 = pltpu.make_async_copy(fresh3, f3_v, l_sem.at[2])
    load_w = pltpu.make_async_copy(weight, w_v.at[0], l_sem.at[3])
    load_pool = pltpu.make_async_copy(pool, pool_v, l_sem.at[4])
    load_res = pltpu.make_async_copy(residual, res_v, l_sem.at[5])
    for load in (load_q, load_f2, load_f3, load_w, load_pool, load_res):
        load.start()

    _, i0, i1, _, _ = scan_leaving(new_slot, req)
    trades, _, _, t0, t1 = scan_leaving(new_slot, partner)
    low, high = jnp.minimum(t0, t1), jnp.maximum(t0, t1)

    load_q.wait()
    load_f2.wait()
    load_f3.wait()
    for k, t in enumerate((t0, t1)):
        new_rows = f3_v[t].astype(jnp.float32)
        qx_s[k, 0:16] = q_v[t]
        qx_s[k, 16:32] = jnp.concatenate(
            [new_rows, jnp.zeros((12, 128), jnp.float32)], 0
        ).astype(jnp.bfloat16)
        qx_s[k, 32:48] = jnp.concatenate(
            [new_rows[2:4], jnp.zeros((14, 128), jnp.float32)], 0
        ).astype(jnp.bfloat16)
    fv_v[...] = pltpu.roll(f2_v[...].astype(jnp.float32), 126, 0).astype(jnp.bfloat16)

    pl.semaphore_wait(barrier, 7 + before)
    for d, a in zip((1, 7, 2, 6), ahead):

        @pl.when(a > 0)
        def _():
            pl.semaphore_signal(ready, inc=1, device_id=at(dz=d), device_id_type=MESH)


    send_q = remote(qx_s, qx_r, qx_sem.at[0], qx_sem.at[1], at(dy=2))
    send_q.start()
    load_w.wait()

    def w_half(d, half):
        return w_v.at[d, pl.ds(half * 512, 512)]

    w_plan = [(0, 3, 1, 0), (1, 1, 3, 1), (1, 3, 1, 2), (0, 1, 3, 3)]
    w_own = [
        remote(w_half(0, half), w_half(d, half), w_ss.at[k], w_rs.at[k], at(dy=dy))
        for half, d, dy, k in w_plan
    ]
    w_own[0].start()
    w_own[1].start()

    t_row = lax.broadcasted_iota(jnp.int32, (128, 256), 0)
    u_col = lax.broadcasted_iota(jnp.int32, (128, 256), 1) & 63
    slot_t = t_row >> 2
    for q in range(4):
        source = x * 8 + core * 4 + q
        _, _, _, a, b = scan_leaving(new_slot, (source + 16) % 32)
        lo, hi = jnp.minimum(a, b), jnp.maximum(a, b)
        last = jnp.where(hi == 30, lo, hi)
        pos = jnp.where(slot_t == 30, lo, slot_t)
        pos = jnp.where(slot_t == 31, last, pos)
        pos = jnp.where(slot_t == lo, 30, pos)
        pos = jnp.where(slot_t == hi, 31, pos)
        row = ((pos >> 3) << 4) + ((t_row & 1) << 3) + (pos & 7)
        for ct in range(2):
            hit = (row == u_col) & (((t_row >> 1) & 1) == ct)
            perm_v[q, ct] = jnp.where(hit, 1.0, 0.0).astype(jnp.bfloat16)

    load_pool.wait()

    scaling = 1.0 / math.sqrt(128)
    lane = lax.broadcasted_iota(jnp.int32, (16, 128), 1)
    odd = (lax.broadcasted_iota(jnp.int32, (16, 128), 0) & 1) == 1

    def attend(requests):
        pages = [[table[p, r[1]] for p in range(5)] for r in requests]
        scores = []
        for (query, old, keys_new, _, place), own in zip(requests, pages):
            span = lengths[req * 32 + old]
            parts = []
            for p in range(5):
                s = dot(query, pool_v[own[p], :, 0:128], NT) * scaling
                parts.append(jnp.where(lane < span - 128 * p, s, NEG_FILL))
            s = dot(query, keys_new, NT) * scaling
            seen = (lane == place) | ((lane == place + 1) & odd)
            parts.append(jnp.where(seen, s, NEG_FILL))
            scores.append(parts)
        tops = [
            jnp.max(functools.reduce(jnp.maximum, parts), axis=1, keepdims=True)
            for parts in scores
        ]
        weights = [[jnp.exp(s - top) for s in parts] for parts, top in zip(scores, tops)]
        totals = [
            jnp.sum(functools.reduce(jnp.add, parts), axis=1, keepdims=True)
            for parts in weights
        ]
        results = []
        for (_, _, _, values_new, _), own, parts in zip(requests, pages, weights):
            mixed = dot(parts[5].astype(jnp.bfloat16), values_new)
            for p in range(5):
                mixed += dot(parts[p].astype(jnp.bfloat16), pool_v[own[p], :, 128:256])
            results.append(mixed)
        return [mixed / total for mixed, total in zip(results, totals)]

    def slot_at(p):
        slot = jnp.where(p == low, jnp.where(high == 30, 31, 30), p)
        slot = jnp.where(p == high, 31, slot)
        slot = jnp.where(p == 30, low, slot)
        return jnp.where(p == 31, high, slot)

    def group(c):
        requests = []
        for k in range(8):
            slot = slot_at(jnp.int32(c * 8 + k))
            v = new_slot[req * 32 + slot]
            old = jnp.where((v >> 5) == req, v & 31, slot)
            requests.append((q_v[slot], old, f2_v[...], fv_v[...], slot * 4))
        for k, result in enumerate(attend(requests)):
            att_v[k * 16 : k * 16 + 16] = result

    def chunk(c):
        return attended.at[z, pl.ds(c * 16, 16)]

    def block(dz, c):
        return attended.at[(z + dz) % 8, pl.ds(c * 16, 16)]

    def publish(c):
        for g in range(8):
            rows = [att_v[pl.ds(2 * g + s, 8, stride=16)] for s in range(2)]
            attended[z, c * 16 : c * 16 + 16, g * 128 : g * 128 + 128] = (
                jnp.concatenate(rows, 0).astype(jnp.bfloat16)
            )
        sends = [
            remote(chunk(c), chunk(c), z_ss.at[c, k], z_rs.at[c, z], at(dz=dz))
            for k, dz in enumerate((1, 7, 2, 6))
        ]
        for k in (2, 3, 0, 1):
            sends[k].start()
        return sends

    def held(source, c):
        return attended.at[source, pl.ds(c * 16, 16)]

    def arrive(source, c):
        remote(
            held(source, c), held(source, c), z_ss.at[c, 0], z_rs.at[c, source], at(dz=1)
        ).wait_recv()

    def z_hop(source, c, n, dz):
        return remote(
            held(source, c), held(source, c), z_ss.at[c, n], z_rs.at[c, source], at(dz=dz)
        )

    def forward(c):
        for here in range(8):

            @pl.when(z == here)
            def _():
                for k, near, n, far, parity in ((6, 1, 4, 2, 0), (2, 7, 5, 6, 1)):
                    source = (here + k) % 8
                    arrive(source, c)
                    z_hop(source, c, n, near).start()
                    if c % 2 == parity:
                        z_hop(source, c, 6, far).start()

        return [z_hop(0, c, n, 1) for n in (4, 5, 6)]

    z_sends = []
    group(0)

    @pl.when(behind > 0)
    def _():
        pl.semaphore_wait(ready, behind)

    z_sends += publish(0)

    send_q.wait_recv()
    pad = jnp.zeros((112, 128), jnp.bfloat16)
    leaving = [
        (
            qx_r[k, 0:16], old,
            jnp.concatenate([qx_r[k, 16:32], pad], 0),
            jnp.concatenate([qx_r[k, 32:48], pad], 0),
            0,
        )
        for k, old in enumerate((i0, i1))
    ]
    for k, result in enumerate(attend(leaving)):
        ret_s[k] = result.astype(jnp.bfloat16)
    send_ret = remote(ret_s, ret_r, ret_sem.at[0], ret_sem.at[1], at(dy=2))
    send_ret.start()
    w_own[2].start()
    w_own[3].start()

    group(1)
    z_sends += publish(1)
    group(2)
    z_sends += publish(2)
    group(3)
    z_sends += forward(0)
    send_ret.wait_recv()
    for p, t in ((6, low), (7, high)):
        came = ret_r[jnp.where(t == t0, 0, 1)].astype(jnp.float32)
        att_v[p * 16 : p * 16 + 16] = jnp.where(
            trades > 0, came, att_v[p * 16 : p * 16 + 16]
        )
    z_sends += publish(3)

    w_fwd = []
    for half, d, dy, k, came in ((0, 3, 1, 4, 0), (1, 1, 3, 5, 1)):
        w_own[came].wait_recv()
        w_fwd.append(
            remote(w_half(d, half), w_half(2, half), w_ss.at[k], w_rs.at[k], at(dy=dy))
        )
        w_fwd[-1].start()
    def source_of(t):
        return t if t < 4 else 11 - t

    def core_copy(t):
        n = t % 4
        return remote(c_s.at[t], c_r.at[n], c_ss.at[n], c_rs.at[n], at(flip=1))

    def y_copy(d, n):
        return remote(
            y_s.at[d, n], y_r.at[d, n], y_ss.at[d, n], y_rs.at[d, n], at(dy=d)
        )

    def x_move(d, n):
        i = (y + 4 - d) % 4
        far = remote(
            y_r.at[d, n], x_r.at[n, x], x_ss.at[d, n], x_rs.at[x, n], (req, i * 2 + core)
        )
        here = pltpu.make_async_copy(y_r.at[d, n], x_r.at[n, x], x_ss.at[d, n])
        return i != x, far, here

    def x_start(d, n):
        other, far, here = x_move(d, n)

        @pl.when(other)
        def _():
            far.start()

        @pl.when(jnp.logical_not(other))
        def _():
            here.start()

    def multiply(t):
        source = source_of(t)
        k = (source + 8 - z) % 8

        @pl.when((k != 0) & (k != 2) & (k != 6))
        def _():
            for c in range(4):
                arrive(source, c)

        rows = attended[source]
        for d in range(4):
            part = dot(rows, w_v[d])
            own_v[t, d] = part
            c_s[t, d] = part.astype(jnp.bfloat16)

        @pl.when(core != t // 4)
        def _():
            core_copy(t).start()

    def join(t):
        n = t % 4

        @pl.when(core == t // 4)
        def _():
            core_copy(t).wait_recv()
            for d in (2, 1, 3, 0):
                both = (own_v[t, d] + c_r[n, d].astype(jnp.float32)).astype(jnp.bfloat16)
                if d == 0:
                    y_r[0, n] = both
                    x_start(0, n)
                else:
                    y_s[d, n] = both
                    y_copy(d, n).start()

    def relay(t):
        @pl.when(core == t // 4)
        def _():
            for d in (1, 3, 2):
                y_copy(d, t % 4).wait_recv()
                x_start(d, t % 4)

    def finish(t):
        n = t % 4
        for k in range(4):

            @pl.when(k != x)
            def _():
                remote(
                    y_r.at[0, n], x_r.at[n, k], x_ss.at[0, n], x_rs.at[k, n], at(dx=1)
                ).wait_recv()

        for d in range(4):
            other, far, here = x_move(d, n)

            @pl.when(other)
            def _():
                far.wait_send()

            @pl.when(jnp.logical_not(other))
            def _():
                here.wait()

        q = source_of(t) - t // 4 * 4
        parts = x_r[n].reshape(256, 256)
        total = dot(perm_v[q, 0], parts[:, 0:128]) + dot(perm_v[q, 1], parts[:, 128:256])
        rows = pl.ds(q * 128, 128)
        total += res_v[rows].astype(jnp.float32)
        out[rows] = total.astype(jnp.bfloat16)

    z_sends += forward(1)
    z_sends += forward(2)
    z_sends += forward(3)
    w_own[2].wait_recv()
    w_own[3].wait_recv()
    for fwd in w_fwd:
        fwd.wait_recv()
    for t in range(8):
        multiply(t)
        if t >= 1:
            join(t - 1)
        if t >= 4:
            relay(t - 4)
    join(7)
    for t in range(4, 8):
        relay(t)

    load_res.wait()
    for first in (0, 4):

        @pl.when(core == first // 4)
        def _():
            for t in range(first, first + 4):
                finish(t)

    send_q.wait_send()
    send_ret.wait_send()
    for send in w_own + w_fwd + z_sends:
        send.wait_send()
    for t in range(8):

        @pl.when(core != t // 4)
        def _():
            core_copy(t).wait_send()

        @pl.when(core == t // 4)
        def _():
            for d in (1, 2, 3):
                y_copy(d, t % 4).wait_send()


def per_device(kv_pool, block_table, lengths, new_slot, queries, new_kv, output_weight, residual):
    q = queries.reshape(32, 2, 8, 128).transpose(0, 2, 1, 3).reshape(32, 16, 128)
    fresh = new_kv.reshape(32, 2, 2, 128).transpose(0, 2, 1, 3)
    res = residual.reshape(128, 2, 2, 128).transpose(0, 2, 1, 3).reshape(512, 128)
    hbm = pl.BlockSpec(memory_space=pl.ANY)
    smem = pl.BlockSpec(memory_space=pltpu.SMEM)
    vmem = pl.BlockSpec(memory_space=pltpu.VMEM)
    bf16, f32 = jnp.bfloat16, jnp.float32
    sem = pltpu.SemaphoreType.DMA
    out = pl.pallas_call(
        kernel,
        name="decode",
        out_shape=pltpu.VMEM((512, 128), bf16),
        in_specs=[hbm] * 6 + [smem] * 3,
        out_specs=vmem,
        scratch_shapes=[
            pltpu.VMEM((160, 128, 256), bf16),
            pltpu.VMEM((4, 1024, 256), bf16),
            pltpu.VMEM((32, 16, 128), bf16),
            pltpu.VMEM((128, 128), bf16),
            pltpu.VMEM((32, 4, 128), bf16),
            pltpu.VMEM((512, 128), bf16),
            pltpu.VMEM((128, 128), bf16),
            pltpu.VMEM((128, 128), f32),
            pltpu.VMEM((8, 64, 1024), bf16),
            pltpu.VMEM((2, 48, 128), bf16),
            pltpu.VMEM((2, 48, 128), bf16),
            pltpu.VMEM((2, 16, 128), bf16),
            pltpu.VMEM((2, 16, 128), bf16),
            pltpu.VMEM((8, 4, 64, 256), bf16),
            pltpu.VMEM((4, 4, 64, 256), bf16),
            pltpu.VMEM((8, 4, 64, 256), f32),
            pltpu.VMEM((4, 4, 64, 256), bf16),
            pltpu.VMEM((4, 4, 64, 256), bf16),
            pltpu.VMEM((4, 4, 64, 256), bf16),
            pltpu.VMEM((4, 2, 128, 256), bf16),
            sem((6,)),
            sem((2,)),
            sem((2,)),
            sem((6,)),
            sem((6,)),
            sem((4, 7)),
            sem((4, 8)),
            sem((4,)),
            sem((4,)),
            sem((4, 4)),
            sem((4, 4)),
            sem((4, 4)),
            sem((4, 4)),
            pltpu.SemaphoreType.REGULAR,
        ],
        compiler_params=pltpu.CompilerParams(
            collective_id=0, has_side_effects=True, vmem_limit_bytes=60 << 20
        ),
    )(
        kv_pool.reshape(160, 128, 256), output_weight, q, fresh.reshape(128, 128),
        fresh.reshape(32, 4, 128), res, block_table.T, lengths, new_slot,
    )
    return out.reshape(128, 2, 2, 128).transpose(0, 2, 1, 3).reshape(128, 2, 256)


def solution(mesh):
    in_specs = (
        P("req", "head", None, None),
        P("req", None),
        P(),
        P(),
        P("req", None, "head"),
        P("req", None, "head", None),
        P("head", "req"),
        P("head", None, "req"),
    )
    return jax.shard_map(
        per_device, mesh=mesh, in_specs=in_specs,
        out_specs=P("head", None, "req"), check_vma=False,
    )
```

```python
import functools
import math

import jax
import jax.numpy as jnp
from jax import lax
from jax.experimental import pallas as pl
from jax.experimental.pallas import tpu as pltpu
from jax.sharding import PartitionSpec as P

MESH = pl.DeviceIdType.MESH
NEG_FILL = -1e30
NT = (((1,), (1,)), ((), ()))
NN = (((1,), (0,)), ((), ()))


def dot(a, b, dims=NN):
    return lax.dot_general(a, b, dims, preferred_element_type=jnp.float32)


def scan_leaving(new_slot, device):
    def body(e, carry):
        count, i0, i1, t0, t1 = carry
        v = new_slot[device * 32 + e]
        leaves = jnp.where((v >> 5) != device, 1, 0)
        first = (leaves == 1) & (count == 0)
        second = (leaves == 1) & (count == 1)
        return (
            count + leaves,
            jnp.where(first, e, i0),
            jnp.where(second, e, i1),
            jnp.where(first, v & 31, t0),
            jnp.where(second, v & 31, t1),
        )

    zero = jnp.int32(0)
    return lax.fori_loop(
        0, 32, body, (zero, zero, zero, jnp.int32(30), jnp.int32(31)), unroll=4
    )


def kernel(
    pool, weight, queries, fresh2, fresh3, residual, table, lengths, new_slot, out,
    pool_v, w_v, q_v, f2_v, f3_v, res_v, fv_v, att_v, attended, qx_s, qx_r, ret_s, ret_r,
    c_s, c_r, own_v, y_s, y_r, x_r, perm_v,
    l_sem, qx_sem, ret_sem, w_ss, w_rs, z_ss, z_rs, c_ss, c_rs, y_ss, y_rs, x_ss, x_rs, ready,
):
    req, head = lax.axis_index("req"), lax.axis_index("head")
    x, core = head // 2, head % 2
    y, z = req // 8, req % 8
    partner = (req + 16) % 32

    def at(dx=0, dy=0, dz=0, flip=0):
        return (
            ((y + dy) % 4) * 8 + (z + dz) % 8,
            ((x + dx) % 4) * 2 + (core + flip) % 2,
        )

    def remote(src, dst, ss, rs, device):
        return pltpu.make_async_remote_copy(
            src_ref=src, dst_ref=dst, send_sem=ss, recv_sem=rs,
            device_id=device, device_id_type=MESH,
        )

    barrier = pltpu.get_barrier_semaphore()
    for peer in [at(dy=d) for d in (1, 3, 2)] + [at(dx=d) for d in (1, 3, 2)] + [at(flip=1)]:
        pl.semaphore_signal(barrier, inc=1, device_id=peer, device_id_type=MESH)

    def rank_of(place):
        return place - (place // 4) * (place - 4)

    rank = rank_of(z)
    ahead = [rank - rank_of((z + d) % 8) for d in (1, 7, 2, 6)]
    before = sum((a + 8) // 8 for a in ahead)
    behind = 4 - before
    for d, a in zip((1, 7, 2, 6), ahead):

        @pl.when(a <= 0)
        def _():
            pl.semaphore_signal(barrier, inc=1, device_id=at(dz=d), device_id_type=MESH)

    load_q = pltpu.make_async_copy(queries, q_v, l_sem.at[0])
    load_f2 = pltpu.make_async_copy(fresh2, f2_v, l_sem.at[1])
    load_f3 = pltpu.make_async_copy(fresh3, f3_v, l_sem.at[2])
    load_w = pltpu.make_async_copy(weight, w_v.at[0], l_sem.at[3])
    load_pool = pltpu.make_async_copy(pool, pool_v, l_sem.at[4])
    load_res = pltpu.make_async_copy(residual, res_v, l_sem.at[5])
    for load in (load_q, load_f2, load_f3, load_w, load_pool, load_res):
        load.start()

    _, i0, i1, _, _ = scan_leaving(new_slot, req)
    trades, _, _, t0, t1 = scan_leaving(new_slot, partner)
    low, high = jnp.minimum(t0, t1), jnp.maximum(t0, t1)

    load_q.wait()
    load_f2.wait()
    load_f3.wait()
    for k, t in enumerate((t0, t1)):
        new_rows = f3_v[t].astype(jnp.float32)
        qx_s[k, 0:16] = q_v[t]
        qx_s[k, 16:32] = jnp.concatenate(
            [new_rows, jnp.zeros((12, 128), jnp.float32)], 0
        ).astype(jnp.bfloat16)
        qx_s[k, 32:48] = jnp.concatenate(
            [new_rows[2:4], jnp.zeros((14, 128), jnp.float32)], 0
        ).astype(jnp.bfloat16)
    fv_v[...] = pltpu.roll(f2_v[...].astype(jnp.float32), 126, 0).astype(jnp.bfloat16)

    pl.semaphore_wait(barrier, 7 + before)
    for d, a in zip((1, 7, 2, 6), ahead):

        @pl.when(a > 0)
        def _():
            pl.semaphore_signal(ready, inc=1, device_id=at(dz=d), device_id_type=MESH)


    send_q = remote(qx_s, qx_r, qx_sem.at[0], qx_sem.at[1], at(dy=2))
    send_q.start()
    load_w.wait()

    def w_half(d, half):
        return w_v.at[d, pl.ds(half * 512, 512)]

    w_plan = [(0, 3, 1, 0), (1, 1, 3, 1), (1, 3, 1, 2), (0, 1, 3, 3)]
    w_own = [
        remote(w_half(0, half), w_half(d, half), w_ss.at[k], w_rs.at[k], at(dy=dy))
        for half, d, dy, k in w_plan
    ]
    w_own[0].start()
    w_own[1].start()

    t_row = lax.broadcasted_iota(jnp.int32, (128, 256), 0)
    u_col = lax.broadcasted_iota(jnp.int32, (128, 256), 1) & 63
    slot_t = t_row >> 2
    for q in range(4):
        source = x * 8 + core * 4 + q
        _, _, _, a, b = scan_leaving(new_slot, (source + 16) % 32)
        lo, hi = jnp.minimum(a, b), jnp.maximum(a, b)
        last = jnp.where(hi == 30, lo, hi)
        pos = jnp.where(slot_t == 30, lo, slot_t)
        pos = jnp.where(slot_t == 31, last, pos)
        pos = jnp.where(slot_t == lo, 30, pos)
        pos = jnp.where(slot_t == hi, 31, pos)
        row = ((pos >> 3) << 4) + ((t_row & 1) << 3) + (pos & 7)
        for ct in range(2):
            hit = (row == u_col) & (((t_row >> 1) & 1) == ct)
            perm_v[q, ct] = jnp.where(hit, 1.0, 0.0).astype(jnp.bfloat16)

    load_pool.wait()

    scaling = 1.0 / math.sqrt(128)
    lane = lax.broadcasted_iota(jnp.int32, (16, 128), 1)
    odd = (lax.broadcasted_iota(jnp.int32, (16, 128), 0) & 1) == 1

    def attend(requests):
        pages = [[table[p, r[1]] for p in range(5)] for r in requests]
        scores = []
        for (query, old, keys_new, _, place), own in zip(requests, pages):
            span = lengths[req * 32 + old]
            parts = []
            for p in range(5):
                s = dot(query, pool_v[own[p], :, 0:128], NT) * scaling
                parts.append(jnp.where(lane < span - 128 * p, s, NEG_FILL))
            s = dot(query, keys_new, NT) * scaling
            seen = (lane == place) | ((lane == place + 1) & odd)
            parts.append(jnp.where(seen, s, NEG_FILL))
            scores.append(parts)
        tops = [
            jnp.max(functools.reduce(jnp.maximum, parts), axis=1, keepdims=True)
            for parts in scores
        ]
        weights = [[jnp.exp(s - top) for s in parts] for parts, top in zip(scores, tops)]
        totals = [
            jnp.sum(functools.reduce(jnp.add, parts), axis=1, keepdims=True)
            for parts in weights
        ]
        results = []
        for (_, _, _, values_new, _), own, parts in zip(requests, pages, weights):
            mixed = dot(parts[5].astype(jnp.bfloat16), values_new)
            for p in range(5):
                mixed += dot(parts[p].astype(jnp.bfloat16), pool_v[own[p], :, 128:256])
            results.append(mixed)
        return [mixed / total for mixed, total in zip(results, totals)]

    def slot_at(p):
        slot = jnp.where(p == low, jnp.where(high == 30, 31, 30), p)
        slot = jnp.where(p == high, 31, slot)
        slot = jnp.where(p == 30, low, slot)
        return jnp.where(p == 31, high, slot)

    def group(c):
        requests = []
        for k in range(8):
            slot = slot_at(jnp.int32(c * 8 + k))
            v = new_slot[req * 32 + slot]
            old = jnp.where((v >> 5) == req, v & 31, slot)
            requests.append((q_v[slot], old, f2_v[...], fv_v[...], slot * 4))
        for k, result in enumerate(attend(requests)):
            att_v[k * 16 : k * 16 + 16] = result

    def chunk(c):
        return attended.at[z, pl.ds(c * 16, 16)]

    def block(dz, c):
        return attended.at[(z + dz) % 8, pl.ds(c * 16, 16)]

    def publish(c):
        for g in range(8):
            rows = [att_v[pl.ds(2 * g + s, 8, stride=16)] for s in range(2)]
            attended[z, c * 16 : c * 16 + 16, g * 128 : g * 128 + 128] = (
                jnp.concatenate(rows, 0).astype(jnp.bfloat16)
            )
        sends = [
            remote(chunk(c), chunk(c), z_ss.at[c, k], z_rs.at[c, z], at(dz=dz))
            for k, dz in enumerate((1, 7, 2, 6))
        ]
        for k in (2, 3, 0, 1):
            sends[k].start()
        return sends

    def held(source, c):
        return attended.at[source, pl.ds(c * 16, 16)]

    def arrive(source, c):
        remote(
            held(source, c), held(source, c), z_ss.at[c, 0], z_rs.at[c, source], at(dz=1)
        ).wait_recv()

    def z_hop(source, c, n, dz):
        return remote(
            held(source, c), held(source, c), z_ss.at[c, n], z_rs.at[c, source], at(dz=dz)
        )

    def forward(c):
        for here in range(8):

            @pl.when(z == here)
            def _():
                for k, near, n, far, parity in ((6, 1, 4, 2, 0), (2, 7, 5, 6, 1)):
                    source = (here + k) % 8
                    arrive(source, c)
                    z_hop(source, c, n, near).start()
                    if c % 2 == parity:
                        z_hop(source, c, 6, far).start()

        return [z_hop(0, c, n, 1) for n in (4, 5, 6)]

    z_sends = []
    group(0)

    @pl.when(behind > 0)
    def _():
        pl.semaphore_wait(ready, behind)

    z_sends += publish(0)
    group(1)
    z_sends += publish(1)

    send_q.wait_recv()
    pad = jnp.zeros((112, 128), jnp.bfloat16)
    leaving = [
        (
            qx_r[k, 0:16], old,
            jnp.concatenate([qx_r[k, 16:32], pad], 0),
            jnp.concatenate([qx_r[k, 32:48], pad], 0),
            0,
        )
        for k, old in enumerate((i0, i1))
    ]
    for k, result in enumerate(attend(leaving)):
        ret_s[k] = result.astype(jnp.bfloat16)
    send_ret = remote(ret_s, ret_r, ret_sem.at[0], ret_sem.at[1], at(dy=2))
    send_ret.start()
    w_own[2].start()
    w_own[3].start()

    group(2)
    z_sends += publish(2)
    group(3)
    z_sends += forward(0)
    send_ret.wait_recv()
    for p, t in ((6, low), (7, high)):
        came = ret_r[jnp.where(t == t0, 0, 1)].astype(jnp.float32)
        att_v[p * 16 : p * 16 + 16] = jnp.where(
            trades > 0, came, att_v[p * 16 : p * 16 + 16]
        )
    z_sends += publish(3)

    w_fwd = []
    for half, d, dy, k, came in ((0, 3, 1, 4, 0), (1, 1, 3, 5, 1)):
        w_own[came].wait_recv()
        w_fwd.append(
            remote(w_half(d, half), w_half(2, half), w_ss.at[k], w_rs.at[k], at(dy=dy))
        )
        w_fwd[-1].start()
    def source_of(t):
        return t if t < 4 else 11 - t

    def core_copy(t):
        n = t % 4
        return remote(c_s.at[t], c_r.at[n], c_ss.at[n], c_rs.at[n], at(flip=1))

    def y_copy(d, n):
        return remote(
            y_s.at[d, n], y_r.at[d, n], y_ss.at[d, n], y_rs.at[d, n], at(dy=d)
        )

    def x_move(d, n):
        i = (y + 4 - d) % 4
        far = remote(
            y_r.at[d, n], x_r.at[n, x], x_ss.at[d, n], x_rs.at[x, n], (req, i * 2 + core)
        )
        here = pltpu.make_async_copy(y_r.at[d, n], x_r.at[n, x], x_ss.at[d, n])
        return i != x, far, here

    def x_start(d, n):
        other, far, here = x_move(d, n)

        @pl.when(other)
        def _():
            far.start()

        @pl.when(jnp.logical_not(other))
        def _():
            here.start()

    def multiply(t):
        source = source_of(t)
        k = (source + 8 - z) % 8

        @pl.when((k != 0) & (k != 2) & (k != 6))
        def _():
            for c in range(4):
                arrive(source, c)

        rows = attended[source]
        for d in range(4):
            part = dot(rows, w_v[d])
            own_v[t, d] = part
            c_s[t, d] = part.astype(jnp.bfloat16)

        @pl.when(core != t // 4)
        def _():
            core_copy(t).start()

    def join(t):
        n = t % 4

        @pl.when(core == t // 4)
        def _():
            core_copy(t).wait_recv()
            for d in (2, 1, 3, 0):
                both = (own_v[t, d] + c_r[n, d].astype(jnp.float32)).astype(jnp.bfloat16)
                if d == 0:
                    y_r[0, n] = both
                    x_start(0, n)
                else:
                    y_s[d, n] = both
                    y_copy(d, n).start()

    def relay(t):
        @pl.when(core == t // 4)
        def _():
            for d in (1, 3, 2):
                y_copy(d, t % 4).wait_recv()
                x_start(d, t % 4)

    def finish(t):
        n = t % 4
        for k in range(4):

            @pl.when(k != x)
            def _():
                remote(
                    y_r.at[0, n], x_r.at[n, k], x_ss.at[0, n], x_rs.at[k, n], at(dx=1)
                ).wait_recv()

        for d in range(4):
            other, far, here = x_move(d, n)

            @pl.when(other)
            def _():
                far.wait_send()

            @pl.when(jnp.logical_not(other))
            def _():
                here.wait()

        q = source_of(t) - t // 4 * 4
        parts = x_r[n].reshape(256, 256)
        total = dot(perm_v[q, 0], parts[:, 0:128]) + dot(perm_v[q, 1], parts[:, 128:256])
        rows = pl.ds(q * 128, 128)
        total += res_v[rows].astype(jnp.float32)
        out[rows] = total.astype(jnp.bfloat16)

    z_sends += forward(1)
    z_sends += forward(2)
    z_sends += forward(3)
    w_own[2].wait_recv()
    w_own[3].wait_recv()
    for fwd in w_fwd:
        fwd.wait_recv()
    for t in range(8):
        multiply(t)
        if t >= 1:
            join(t - 1)
    join(7)
    for t in range(8):
        relay(t)

    load_res.wait()
    for first in (0, 4):

        @pl.when(core == first // 4)
        def _():
            for t in range(first, first + 4):
                finish(t)

    send_q.wait_send()
    send_ret.wait_send()
    for send in w_own + w_fwd + z_sends:
        send.wait_send()
    for t in range(8):

        @pl.when(core != t // 4)
        def _():
            core_copy(t).wait_send()

        @pl.when(core == t // 4)
        def _():
            for d in (1, 2, 3):
                y_copy(d, t % 4).wait_send()


def per_device(kv_pool, block_table, lengths, new_slot, queries, new_kv, output_weight, residual):
    q = queries.reshape(32, 2, 8, 128).transpose(0, 2, 1, 3).reshape(32, 16, 128)
    fresh = new_kv.reshape(32, 2, 2, 128).transpose(0, 2, 1, 3)
    res = residual.reshape(128, 2, 2, 128).transpose(0, 2, 1, 3).reshape(512, 128)
    hbm = pl.BlockSpec(memory_space=pl.ANY)
    smem = pl.BlockSpec(memory_space=pltpu.SMEM)
    vmem = pl.BlockSpec(memory_space=pltpu.VMEM)
    bf16, f32 = jnp.bfloat16, jnp.float32
    sem = pltpu.SemaphoreType.DMA
    out = pl.pallas_call(
        kernel,
        name="decode",
        out_shape=pltpu.VMEM((512, 128), bf16),
        in_specs=[hbm] * 6 + [smem] * 3,
        out_specs=vmem,
        scratch_shapes=[
            pltpu.VMEM((160, 128, 256), bf16),
            pltpu.VMEM((4, 1024, 256), bf16),
            pltpu.VMEM((32, 16, 128), bf16),
            pltpu.VMEM((128, 128), bf16),
            pltpu.VMEM((32, 4, 128), bf16),
            pltpu.VMEM((512, 128), bf16),
            pltpu.VMEM((128, 128), bf16),
            pltpu.VMEM((128, 128), f32),
            pltpu.VMEM((8, 64, 1024), bf16),
            pltpu.VMEM((2, 48, 128), bf16),
            pltpu.VMEM((2, 48, 128), bf16),
            pltpu.VMEM((2, 16, 128), bf16),
            pltpu.VMEM((2, 16, 128), bf16),
            pltpu.VMEM((8, 4, 64, 256), bf16),
            pltpu.VMEM((4, 4, 64, 256), bf16),
            pltpu.VMEM((8, 4, 64, 256), f32),
            pltpu.VMEM((4, 4, 64, 256), bf16),
            pltpu.VMEM((4, 4, 64, 256), bf16),
            pltpu.VMEM((4, 4, 64, 256), bf16),
            pltpu.VMEM((4, 2, 128, 256), bf16),
            sem((6,)),
            sem((2,)),
            sem((2,)),
            sem((6,)),
            sem((6,)),
            sem((4, 7)),
            sem((4, 8)),
            sem((4,)),
            sem((4,)),
            sem((4, 4)),
            sem((4, 4)),
            sem((4, 4)),
            sem((4, 4)),
            pltpu.SemaphoreType.REGULAR,
        ],
        compiler_params=pltpu.CompilerParams(
            collective_id=0, has_side_effects=True, vmem_limit_bytes=60 << 20
        ),
    )(
        kv_pool.reshape(160, 128, 256), output_weight, q, fresh.reshape(128, 128),
        fresh.reshape(32, 4, 128), res, block_table.T, lengths, new_slot,
    )
    return out.reshape(128, 2, 2, 128).transpose(0, 2, 1, 3).reshape(128, 2, 256)


def solution(mesh):
    in_specs = (
        P("req", "head", None, None),
        P("req", None),
        P(),
        P(),
        P("req", None, "head"),
        P("req", None, "head", None),
        P("head", "req"),
        P("head", None, "req"),
    )
    return jax.shard_map(
        per_device, mesh=mesh, in_specs=in_specs,
        out_specs=P("head", None, "req"), check_vma=False,
    )
```
